32 devices in a mesh: groups: 2 (over y), expert: 4 (over z), tensor: 4 (over x, core).
Axes of the slice: x: 2, y: 2, z: 4, core: 2. Of those that a mesh axis runs over, the one named last changes fastest.
Arguments:
- tokens: bfloat16 [2048, 1440], P(('groups', 'expert'), 'tensor'), parts along dimension 0, may hold values from -6 to 6
- out_grad: bfloat16 [2048, 1440], P(('groups', 'expert'), 'tensor'), parts along dimension 0, may hold values from -6 to 6
- routes: int32 [2048, 2], P(('groups', 'expert')), parts along dimension 0, may hold values from 0 to 3, all different within a row; in each aligned block of 256 rows (0 to 255, 256 to 511, ...) at most 256 rows name the same one
- route_probs: bfloat16 [2048, 2], P(('groups', 'expert')), parts along dimension 0, may hold values from 0.049804688 to 1
- w_gate: bfloat16 [4, 1440, 1440], P('expert', None, 'tensor'), may hold values from -0.21875 to 0.21875
- w_up: bfloat16 [4, 1440, 1440], P('expert', None, 'tensor'), may hold values from -0.21875 to 0.21875
- w_down: bfloat16 [4, 1440, 1440], P('expert', 'tensor'), may hold values from -0.15625 to 0.15625
Outputs:
- grad_tokens: bfloat16 [2048, 1440], P(('groups', 'expert'), 'tensor'), parts along dimension 0
- grad_gate: bfloat16 [8, 1440, 1440], P(('groups', 'expert'), None, 'tensor'), parts along dimension 0
- grad_up: bfloat16 [8, 1440, 1440], P(('groups', 'expert'), None, 'tensor'), parts along dimension 0
- grad_down: bfloat16 [8, 1440, 1440], P(('groups', 'expert'), 'tensor'), parts along dimension 0
The draws below stay inside these ranges and needn't reach their ends.
There are 2 independent parts, one for each index of `groups`. The reference program is written for one: setup_inputs(seed, part) draws one part's arguments, and reference() takes and returns one part's arrays. A program takes and returns all parts, laid end to end along the dimension named above; an argument that names none is the same for every part. Nothing has to cross between parts.
Inputs may be any that keep to these rules, and one draw needn't show every extreme that they name: In the rows of one device (aligned blocks of 256 tokens) no expert is named by more than 256 routes; the 2 ids of a token differ.
All inputs are finite; a program needn't handle non-finite values.
Results may differ from the reference program's by a relative error of at most 0.01.
Values may be sent and summed in bfloat16 or wider, within the bound.
No kernel may reach another device: no remote copies, remote signals or barrier semaphores. Data moves between devices by JAX's collectives and lax.ppermute only.
A program may use at most 64 MiB of HBM per device.

```python
import math
import jax
import jax.numpy as jnp
import numpy as np
from jax import lax

D = 1440
FF = 1440
TOP = 2
TOK_DEV = 256
EXPERTS = 4
TOKENS = 1024
CAP = 1024
SLOT = 256
N_TENSOR = 4


def with_spikes(drawn, own_key, source, target, blocks, factor):
    def block_of(dim):
        return (jnp.arange(drawn.shape[dim]) // (drawn.shape[dim] // blocks)).reshape((-1,) + (1,) * (drawn.ndim - 1 - dim))

    first = jax.random.permutation(own_key, blocks)[block_of(target)]
    far = (block_of(target) + blocks // 2) % blocks
    return jnp.where((block_of(source) == first) | (block_of(source) == far), factor * drawn, drawn)


def level_of(rng, dims, split, least, largest):
    level, own = 1.0, jax.random.fold_in(rng, 6)
    for dim, parts in split:
        heights = jnp.exp(jax.random.uniform(jax.random.fold_in(own, dim), (parts,), jnp.float32, least / len(split), largest / len(split)))
        level = level * jnp.repeat(heights, dims[dim] // parts).reshape([-1 if axis == dim else 1 for axis in range(len(dims))])
    return level


def routed_block(stream_key, own, number, rows, number_of, top, reach, skew):
    ranking = jax.random.permutation(stream_key, number_of)
    heavy_load, usual = portions_of(number_of, rows * top, reach, skew, True), portions_of(number_of, rows * top, reach, skew, False)
    places = jnp.arange(number_of)

    def named(tallies, turn):
        used = int((tallies > 0).sum())
        fixed = max(1, used // 4)
        shifted = fixed + (places - fixed + turn * (used - fixed)) % max(1, number_of - fixed)
        return jnp.zeros((number_of,), jnp.int32).at[ranking[jnp.where(places < fixed, places, shifted)]].set(jnp.asarray(tallies, jnp.int32))

    tallies = jnp.where(number % 4 == 0, named(heavy_load, number // 4), named(usual, number - number // 4 - 1))
    mixed = jax.random.permutation(jax.random.fold_in(own, 3), number_of)
    donor, sink = mixed[0:number_of // 2 * 2:2], mixed[1:number_of // 2 * 2:2]
    room = jnp.minimum(tallies[donor] - 1, reach - tallies[sink]) // 2
    room = jnp.where((donor == ranking[0]) | (sink == ranking[0]) | (tallies[sink] == 0), 0, jnp.maximum(room, 0))
    shifted = jax.random.randint(jax.random.fold_in(own, 4), (number_of // 2,), 0, 1 << 20) % (room + 1)
    tallies = tallies.at[donor].add(-shifted).at[sink].add(shifted)
    items = jnp.searchsorted(jnp.cumsum(tallies), jnp.arange(rows * top), side="right").astype(jnp.int32)
    listing = items.reshape(top, rows).T
    listing = listing[jax.random.permutation(jax.random.fold_in(own, 1), rows)]
    turn = jax.random.randint(jax.random.fold_in(own, 2), (rows, 1), 0, top)
    return jnp.take_along_axis(listing, (jnp.arange(top)[None, :] + turn) % top, axis=1)


def portions_of(number_of, total, limit, lean, full):
    portions = [(1 << 20) // math.isqrt(standing ** lean) + 1 for standing in range(1, number_of + 1)]
    largest = limit if full else min(limit, max(-(-total // number_of), total * portions[0] // sum(portions)))
    least = 1 if total - largest >= number_of - 1 else 0
    given, surplus = [largest] + [least] * (number_of - 1), total - largest - least * (number_of - 1)
    while surplus > 0:
        movable = [i for i in range(1, number_of) if given[i] < largest] or [i for i in range(1, number_of) if given[i] < limit]
        whole, left = sum([portions[i] for i in movable]), surplus
        for i in movable:
            more = min(limit - given[i], max(1, left * portions[i] // whole), surplus)
            given[i] = given[i] + more
            surplus = surplus - more
    return np.array(given)


def noise(key, dims, width, limit, pieces=(), held_as=jnp.bfloat16):
    level = level_of(key, dims, pieces, -0.22, 0.18) if pieces else 1.0
    drawn = jax.random.normal(key, dims, jnp.float32) * width * level
    return jnp.minimum(jnp.maximum(drawn, -limit), limit).astype(held_as)


def noise_with(stream_key, shape, scale, bound, cuts, heavy, kind=jnp.bfloat16):
    result = scale * jax.random.normal(stream_key, shape, jnp.float32)
    if cuts:
        result = result * level_of(stream_key, shape, cuts, -0.22, 0.18)
    return jnp.clip(with_spikes(result, jax.random.fold_in(stream_key, 3), *heavy), -bound, bound).astype(kind)


def setup_inputs(seed: int = 0, part: int = 0) -> dict:
    seeds = jax.random.split(jax.random.key(seed), 8)
    own_keys = jax.random.split(jax.random.fold_in(seeds[7], part), 8)
    tokens = noise(own_keys[0], (TOKENS, D), 1.0, 6.0, ((0, 4), (1, 4)))
    out_grad = noise(own_keys[1], (TOKENS, D), 1.0, 6.0, ((0, 4), (1, 4)))
    routes_keys = jax.random.split(jax.random.fold_in(own_keys[2], 1), TOKENS // TOK_DEV)
    routes_turns = jax.random.permutation(jax.random.fold_in(own_keys[2], 3), TOKENS // TOK_DEV)
    routes = jax.vmap(lambda own, number: routed_block(jax.random.fold_in(own_keys[2], 2), own, number, TOK_DEV, EXPERTS, TOP, SLOT, 2))(routes_keys, routes_turns).reshape((TOKENS, TOP))
    route_probs = jnp.clip(jnp.exp(math.log(1.0) - 2.9996462 * jax.random.uniform(own_keys[3], (TOKENS, TOP), jnp.float32) ** level_of(own_keys[3], (TOKENS, TOP), ((0, 4),), -0.2, 0.2)), 0.049804688, 1.0).astype(jnp.bfloat16)
    w_gate = noise_with(seeds[4], (EXPERTS, D, FF), D ** -0.5, 0.21875, ((0, 4), (2, 4)), (2, 1, 4, 2.0))
    w_up = noise_with(seeds[5], (EXPERTS, D, FF), D ** -0.5, 0.21875, ((0, 4), (2, 4)), (2, 1, 4, 2.0))
    w_down = noise(seeds[6], (EXPERTS, FF, D), FF ** -0.5, 0.15625, ((0, 4), (1, 4)))
    return {"tokens": tokens, "out_grad": out_grad, "routes": routes, "route_probs": route_probs, "w_gate": w_gate, "w_up": w_up, "w_down": w_down}


def expert_rows(flat_ids, expert):
    count = flat_ids.shape[0]
    routed = flat_ids == expert
    position = jnp.cumsum(routed.astype(jnp.int32)) - 1
    target = jnp.where(routed, position, CAP).astype(jnp.int32)
    empty = jnp.full((CAP,), count, jnp.int32)
    return empty.at[target].set(jnp.arange(count, dtype=jnp.int32), mode="drop")


def reference(tokens, out_grad, routes, route_probs, w_gate, w_up, w_down):
    route_total = TOKENS * TOP
    block_width = FF // N_TENSOR
    flat_ids = routes.reshape(-1).astype(jnp.int32)
    flat_token = jnp.concatenate([jnp.arange(route_total, dtype=jnp.int32) // TOP, jnp.full((1,), TOKENS, jnp.int32)])
    padded_tokens = jnp.concatenate([tokens, jnp.zeros((1, D), tokens.dtype)])
    padded_grads = jnp.concatenate([out_grad, jnp.zeros((1, D), out_grad.dtype)])
    padded_probs = jnp.concatenate([route_probs.reshape(-1), jnp.zeros((1,), route_probs.dtype)])

    def expert_step(collected, expert):
        source_row = expert_rows(flat_ids, expert)
        token_row = flat_token[source_row]
        rows_x = padded_tokens[token_row]
        rows_dy = padded_grads[token_row]
        weight_row = padded_probs[source_row].astype(jnp.float32)[:, None]
        gate_weight = w_gate[expert]
        up_weight = w_up[expert]
        down_weight = w_down[expert]
        pre_gate = jnp.dot(rows_x, gate_weight, preferred_element_type=jnp.float32)
        pre_up = jnp.dot(rows_x, up_weight, preferred_element_type=jnp.float32)
        hidden_grad = jnp.dot(rows_dy, down_weight.T, preferred_element_type=jnp.float32) * weight_row
        sigmoid_gate = jax.nn.sigmoid(pre_gate)
        activated = pre_gate * sigmoid_gate
        hidden = activated * pre_up
        grad_gate_pre = (hidden_grad * pre_up * sigmoid_gate * (1.0 + pre_gate * (1.0 - sigmoid_gate))).astype(jnp.bfloat16)
        grad_up_pre = (hidden_grad * activated).astype(jnp.bfloat16)
        scaled_hidden = (hidden * weight_row).astype(jnp.bfloat16)
        partial_gate = jnp.einsum("cnf,dnf->ncd", grad_gate_pre.astype(jnp.float32).reshape(CAP, N_TENSOR, block_width), gate_weight.astype(jnp.float32).reshape(D, N_TENSOR, block_width), precision=lax.Precision.HIGHEST)
        partial_up = jnp.einsum("cnf,dnf->ncd", grad_up_pre.astype(jnp.float32).reshape(CAP, N_TENSOR, block_width), up_weight.astype(jnp.float32).reshape(D, N_TENSOR, block_width), precision=lax.Precision.HIGHEST)
        blocks = (partial_gate + partial_up).astype(jnp.bfloat16)
        blocks = lax.optimization_barrier(blocks)
        route_grad = jnp.sum(blocks.astype(jnp.float32), axis=0).astype(jnp.bfloat16)
        collected = collected.at[source_row].set(route_grad)
        gate_grad = jnp.dot(rows_x.T, grad_gate_pre, preferred_element_type=jnp.float32).astype(jnp.bfloat16)
        up_grad = jnp.dot(rows_x.T, grad_up_pre, preferred_element_type=jnp.float32).astype(jnp.bfloat16)
        down_grad = jnp.dot(scaled_hidden.T, rows_dy, preferred_element_type=jnp.float32).astype(jnp.bfloat16)
        return collected, (gate_grad, up_grad, down_grad)

    initial = jnp.zeros((route_total + 1, D), jnp.bfloat16)
    collected, grads = lax.scan(expert_step, initial, jnp.arange(EXPERTS, dtype=jnp.int32))
    per_route = collected[:route_total].astype(jnp.float32).reshape(TOKENS, TOP, D)
    grad_tokens = jnp.sum(per_route, axis=1).astype(jnp.bfloat16)
    return grad_tokens, grads[0], grads[1], grads[2]
```

```python
import jax
import jax.numpy as jnp
from jax import lax
from jax.sharding import PartitionSpec as P


def per_device_routed(tokens, out_grad, routes, route_probs, w_gate, w_up, w_down):
    expert_count = lax.axis_size("expert")
    token_count, route_count = routes.shape
    route_total = token_count * route_count
    capacity = 2 * route_total
    slot_size = capacity // expert_count
    flat_ids = routes.reshape(-1)
    onehot = (flat_ids[:, None] == jnp.arange(expert_count, dtype=jnp.int32)[None, :]).astype(
        jnp.int32
    )
    before = jnp.cumsum(onehot, axis=0) - onehot
    position = jnp.sum(before * onehot, axis=1)
    slot_of_route = flat_ids * slot_size + position
    route_of_slot = (
        jnp.full((capacity,), route_total, jnp.int32)
        .at[slot_of_route]
        .set(jnp.arange(route_total, dtype=jnp.int32))
    )
    token_of_slot = route_of_slot // route_count
    weights_send = jnp.take(
        jnp.concatenate([route_probs.reshape(-1), jnp.zeros((1,), route_probs.dtype)]),
        route_of_slot,
        axis=0,
    )

    def spread(block_rows):
        padded = jnp.concatenate(
            [block_rows, jnp.zeros((1, block_rows.shape[1]), block_rows.dtype)]
        )
        return jnp.take(padded, token_of_slot, axis=0)

    full_x, full_dy = (
        lax.all_gather(tokens, "tensor", axis=1, tiled=True),
        lax.all_gather(out_grad, "tensor", axis=1, tiled=True),
    )
    rows_x, rows_dy, rows_weight = (
        lax.all_to_all(spread(full_x), "expert", split_axis=0, concat_axis=0, tiled=True),
        lax.all_to_all(spread(full_dy), "expert", split_axis=0, concat_axis=0, tiled=True),
        lax.all_to_all(weights_send, "expert", split_axis=0, concat_axis=0, tiled=True),
    )
    gate_weight = w_gate[0]
    up_weight = w_up[0]
    down_weight = w_down[0]
    contract_last = (((1,), (1,)), ((), ()))
    contract_rows = (((0,), (0,)), ((), ()))
    weight_row = rows_weight.astype(jnp.float32)[:, None]
    pre_gate = jnp.dot(rows_x, gate_weight, preferred_element_type=jnp.float32)
    pre_up = jnp.dot(rows_x, up_weight, preferred_element_type=jnp.float32)
    hidden_grad = (
        lax.dot_general(rows_dy, down_weight, contract_last, preferred_element_type=jnp.float32)
        * weight_row
    )
    sigmoid_gate = jax.nn.sigmoid(pre_gate)
    activated = pre_gate * sigmoid_gate
    hidden = activated * pre_up
    grad_gate_pre = (
        hidden_grad * pre_up * sigmoid_gate * (1.0 + pre_gate * (1.0 - sigmoid_gate))
    ).astype(jnp.bfloat16)
    grad_up_pre = (hidden_grad * activated).astype(jnp.bfloat16)
    scaled_hidden = (hidden * weight_row).astype(jnp.bfloat16)
    partials = lax.dot_general(
        grad_gate_pre, gate_weight, contract_last, preferred_element_type=jnp.float32
    )
    partials = partials + lax.dot_general(
        grad_up_pre, up_weight, contract_last, preferred_element_type=jnp.float32
    )
    partials = partials.astype(jnp.bfloat16)
    summed = (
        lax.psum_scatter(partials, "tensor", scatter_dimension=1, tiled=True)
        .astype(jnp.float32)
        .astype(jnp.bfloat16)
    )
    returned = lax.all_to_all(summed, "expert", split_axis=0, concat_axis=0, tiled=True)
    per_route = (
        jnp.take(returned, slot_of_route, axis=0)
        .astype(jnp.float32)
        .reshape(token_count, route_count, -1)
    )
    grad_tokens = jnp.sum(per_route, axis=1).astype(jnp.bfloat16)
    grad_gate = lax.dot_general(
        rows_x, grad_gate_pre, contract_rows, preferred_element_type=jnp.float32
    ).astype(jnp.bfloat16)
    grad_up = lax.dot_general(
        rows_x, grad_up_pre, contract_rows, preferred_element_type=jnp.float32
    ).astype(jnp.bfloat16)
    grad_down = lax.dot_general(
        scaled_hidden, rows_dy, contract_rows, preferred_element_type=jnp.float32
    ).astype(jnp.bfloat16)
    return (grad_tokens, grad_gate[None], grad_up[None], grad_down[None])


F32 = jnp.float32
BF16 = jnp.bfloat16


def swap(block, axis, bit):
    size = lax.axis_size(axis)
    return lax.ppermute(block, axis, [(i, i ^ bit) for i in range(size)])


def in_order(pieces, me):
    stacked = jnp.stack(pieces)
    return jnp.concatenate(
        [lax.dynamic_index_in_dim(stacked, me ^ t, 0, keepdims=False) for t in range(len(pieces))]
    )


def add(a, b):
    return (a.astype(F32) + b.astype(F32)).astype(BF16)


def per_device(tokens, out_grad, routes, route_probs, w_gate, w_up, w_down):
    experts, partners = lax.axis_size("expert"), lax.axis_size("tensor")
    token_count, route_count = routes.shape
    if experts != 4 or partners != 4:
        return per_device_routed(tokens, out_grad, routes, route_probs, w_gate, w_up, w_down)
    width = tokens.shape[1]
    me = lax.axis_index("tensor")
    here = lax.axis_index("expert")

    named = routes[:, :, None] == jnp.arange(experts, dtype=jnp.int32)[None, None, :]
    by_expert = jnp.sum(jnp.where(named, route_probs.astype(F32)[:, :, None], 0.0), axis=1)
    weights = jnp.zeros((16, token_count), BF16).at[:experts].set(by_expert.T.astype(BF16))
    own = jnp.concatenate([tokens.T, out_grad.T, weights])

    z1 = swap(own, "expert", 1)
    z2 = swap(own, "expert", 2)
    z3 = swap(z2, "expert", 1)

    gate_t = w_gate[0].T
    up_t = w_up[0].T
    down = w_down[0]
    both = jnp.concatenate([w_gate[0], w_up[0]], axis=1)

    def forward(block):
        far = swap(block, "tensor", 2)
        near = swap(block, "tensor", 1)
        diagonal = swap(far, "tensor", 1)
        pieces = (block, near, far, diagonal)
        x = in_order([p[:width] for p in pieces], me)
        dy = in_order([p[width : 2 * width] for p in pieces], me)
        weight = lax.dynamic_slice_in_dim(block, 2 * width + here, 1, 0).astype(F32)
        pre_gate = jnp.dot(gate_t, x, preferred_element_type=F32)
        pre_up = jnp.dot(up_t, x, preferred_element_type=F32)
        hidden_grad = jnp.dot(down, dy, preferred_element_type=F32) * weight
        sigmoid_gate = jax.nn.sigmoid(pre_gate)
        activated = pre_gate * sigmoid_gate
        grad_gate_pre = (
            hidden_grad * pre_up * sigmoid_gate * (1.0 + pre_gate * (1.0 - sigmoid_gate))
        ).astype(BF16)
        grad_up_pre = (hidden_grad * activated).astype(BF16)
        scaled_hidden = (activated * pre_up * weight).astype(BF16)
        grads = jnp.concatenate([grad_gate_pre, grad_up_pre])
        partial = jnp.dot(both, grads, preferred_element_type=F32).astype(BF16)
        partial = partial.reshape(partners, width, token_count)
        mine = [lax.dynamic_index_in_dim(partial, me ^ k, 0, keepdims=False) for k in range(4)]
        got = swap(jnp.stack([mine[1], mine[3]]), "tensor", 1)
        kept = add(mine[0], got[0])
        sent = add(mine[2], got[1])
        summed = add(kept, swap(sent, "tensor", 2))
        return x, dy, grads, scaled_hidden, summed

    parts = [forward(b) for b in (own, z1, z2, z3)]
    s0, s1, s2, s3 = [p[4] for p in parts]
    t0 = s0.astype(F32) + swap(s1, "expert", 1).astype(F32)
    t2 = add(s2, swap(s3, "expert", 1))
    grad_tokens = (t0 + swap(t2, "expert", 2).astype(F32)).astype(BF16).T

    parts = lax.optimization_barrier([p[:4] for p in parts])
    x, dy, grads, scaled = [jnp.concatenate([p[i] for p in parts], axis=1) for i in range(4)]
    lanes = (((1,), (1,)), ((), ()))
    half = grads.shape[0] // 2
    grad_gate = lax.dot_general(x, grads[:half], lanes, preferred_element_type=F32).astype(BF16)
    grad_up = lax.dot_general(x, grads[half:], lanes, preferred_element_type=F32).astype(BF16)
    grad_down = lax.dot_general(scaled, dy, lanes, preferred_element_type=F32).astype(BF16)
    return (grad_tokens, grad_gate[None], grad_up[None], grad_down[None])


def solution(mesh):
    placed = (
        P(("groups", "expert"), "tensor"),
        P(("groups", "expert"), "tensor"),
        P(("groups", "expert"), None),
        P(("groups", "expert"), None),
        P("expert", None, "tensor"),
        P("expert", None, "tensor"),
        P("expert", "tensor", None),
    )
    return jax.shard_map(
        per_device,
        mesh=mesh,
        in_specs=placed,
        out_specs=(
            P(("groups", "expert"), "tensor"),
            P(("groups", "expert"), None, "tensor"),
            P(("groups", "expert"), None, "tensor"),
            P(("groups", "expert"), "tensor", None),
        ),
        check_vma=False,
    )
```

```python
import jax
import jax.numpy as jnp
from jax import lax
from jax.sharding import PartitionSpec as P


def per_device_routed(tokens, out_grad, routes, route_probs, w_gate, w_up, w_down):
    expert_count = lax.axis_size("expert")
    token_count, route_count = routes.shape
    route_total = token_count * route_count
    capacity = 2 * route_total
    slot_size = capacity // expert_count
    flat_ids = routes.reshape(-1)
    onehot = (flat_ids[:, None] == jnp.arange(expert_count, dtype=jnp.int32)[None, :]).astype(
        jnp.int32
    )
    before = jnp.cumsum(onehot, axis=0) - onehot
    position = jnp.sum(before * onehot, axis=1)
    slot_of_route = flat_ids * slot_size + position
    route_of_slot = (
        jnp.full((capacity,), route_total, jnp.int32)
        .at[slot_of_route]
        .set(jnp.arange(route_total, dtype=jnp.int32))
    )
    token_of_slot = route_of_slot // route_count
    weights_send = jnp.take(
        jnp.concatenate([route_probs.reshape(-1), jnp.zeros((1,), route_probs.dtype)]),
        route_of_slot,
        axis=0,
    )

    def spread(block_rows):
        padded = jnp.concatenate(
            [block_rows, jnp.zeros((1, block_rows.shape[1]), block_rows.dtype)]
        )
        return jnp.take(padded, token_of_slot, axis=0)

    full_x, full_dy = (
        lax.all_gather(tokens, "tensor", axis=1, tiled=True),
        lax.all_gather(out_grad, "tensor", axis=1, tiled=True),
    )
    rows_x, rows_dy, rows_weight = (
        lax.all_to_all(spread(full_x), "expert", split_axis=0, concat_axis=0, tiled=True),
        lax.all_to_all(spread(full_dy), "expert", split_axis=0, concat_axis=0, tiled=True),
        lax.all_to_all(weights_send, "expert", split_axis=0, concat_axis=0, tiled=True),
    )
    gate_weight = w_gate[0]
    up_weight = w_up[0]
    down_weight = w_down[0]
    contract_last = (((1,), (1,)), ((), ()))
    contract_rows = (((0,), (0,)), ((), ()))
    weight_row = rows_weight.astype(jnp.float32)[:, None]
    pre_gate = jnp.dot(rows_x, gate_weight, preferred_element_type=jnp.float32)
    pre_up = jnp.dot(rows_x, up_weight, preferred_element_type=jnp.float32)
    hidden_grad = (
        lax.dot_general(rows_dy, down_weight, contract_last, preferred_element_type=jnp.float32)
        * weight_row
    )
    sigmoid_gate = jax.nn.sigmoid(pre_gate)
    activated = pre_gate * sigmoid_gate
    hidden = activated * pre_up
    grad_gate_pre = (
        hidden_grad * pre_up * sigmoid_gate * (1.0 + pre_gate * (1.0 - sigmoid_gate))
    ).astype(jnp.bfloat16)
    grad_up_pre = (hidden_grad * activated).astype(jnp.bfloat16)
    scaled_hidden = (hidden * weight_row).astype(jnp.bfloat16)
    partials = lax.dot_general(
        grad_gate_pre, gate_weight, contract_last, preferred_element_type=jnp.float32
    )
    partials = partials + lax.dot_general(
        grad_up_pre, up_weight, contract_last, preferred_element_type=jnp.float32
    )
    partials = partials.astype(jnp.bfloat16)
    summed = (
        lax.psum_scatter(partials, "tensor", scatter_dimension=1, tiled=True)
        .astype(jnp.float32)
        .astype(jnp.bfloat16)
    )
    returned = lax.all_to_all(summed, "expert", split_axis=0, concat_axis=0, tiled=True)
    per_route = (
        jnp.take(returned, slot_of_route, axis=0)
        .astype(jnp.float32)
        .reshape(token_count, route_count, -1)
    )
    grad_tokens = jnp.sum(per_route, axis=1).astype(jnp.bfloat16)
    grad_gate = lax.dot_general(
        rows_x, grad_gate_pre, contract_rows, preferred_element_type=jnp.float32
    ).astype(jnp.bfloat16)
    grad_up = lax.dot_general(
        rows_x, grad_up_pre, contract_rows, preferred_element_type=jnp.float32
    ).astype(jnp.bfloat16)
    grad_down = lax.dot_general(
        scaled_hidden, rows_dy, contract_rows, preferred_element_type=jnp.float32
    ).astype(jnp.bfloat16)
    return (grad_tokens, grad_gate[None], grad_up[None], grad_down[None])


F32 = jnp.float32
BF16 = jnp.bfloat16


def swap(block, axis, bit):
    size = lax.axis_size(axis)
    return lax.ppermute(block, axis, [(i, i ^ bit) for i in range(size)])


def in_order(pieces, me):
    stacked = jnp.stack(pieces)
    return jnp.concatenate(
        [lax.dynamic_index_in_dim(stacked, me ^ t, 0, keepdims=False) for t in range(len(pieces))]
    )


def add(a, b):
    return (a.astype(F32) + b.astype(F32)).astype(BF16)


def after(value, *others):
    head = value[:16].astype(F32)
    for other in others:
        zero = other[:16, :1].astype(F32)
        head = head + jnp.where(zero > 3e38, zero, 0.0)
    return lax.dynamic_update_slice(value, head.astype(value.dtype), (0,) * value.ndim)


def per_device(tokens, out_grad, routes, route_probs, w_gate, w_up, w_down):
    experts, partners = lax.axis_size("expert"), lax.axis_size("tensor")
    token_count, route_count = routes.shape
    if experts != 4 or partners != 4:
        return per_device_routed(tokens, out_grad, routes, route_probs, w_gate, w_up, w_down)
    width = tokens.shape[1]
    me = lax.axis_index("tensor")
    here = lax.axis_index("expert")

    ids, probs = routes.T[:, None, :], route_probs.T[:, None, :]
    expert = lax.broadcasted_iota(jnp.int32, (route_count, 16, token_count), 1)
    weights = jnp.sum(jnp.where(ids == expert, probs, jnp.zeros((), BF16)), axis=0)
    own = jnp.concatenate([tokens.T, out_grad.T, weights])

    gate, up, down = w_gate[0], w_up[0], w_down[0]
    both = jnp.concatenate([gate, up], axis=1)
    first = (((0,), (0,)), ((), ()))
    lanes = (((1,), (1,)), ((), ()))

    def forward(block, near, far, diagonal):
        pieces = (block, near, far, diagonal)
        x = in_order([p[:width] for p in pieces], me)
        dy = in_order([p[width : 2 * width] for p in pieces], me)
        weight = lax.dynamic_slice_in_dim(block, 2 * width + here, 1, 0).astype(F32)
        pre_gate = lax.dot_general(gate, x, first, preferred_element_type=F32)
        pre_up = lax.dot_general(up, x, first, preferred_element_type=F32)
        hidden_grad = jnp.dot(down, dy, preferred_element_type=F32) * weight
        sigmoid_gate = jax.nn.sigmoid(pre_gate)
        activated = pre_gate * sigmoid_gate
        grad_gate_pre = (
            hidden_grad * pre_up * sigmoid_gate * (1.0 + pre_gate * (1.0 - sigmoid_gate))
        ).astype(BF16)
        grad_up_pre = (hidden_grad * activated).astype(BF16)
        scaled_hidden = (activated * pre_up * weight).astype(BF16)
        grads = jnp.concatenate([grad_gate_pre, grad_up_pre])
        partial = jnp.dot(both, grads, preferred_element_type=F32).astype(BF16)
        partial = partial.reshape(partners, width, token_count)
        mine = [lax.dynamic_index_in_dim(partial, me ^ k, 0, keepdims=False) for k in range(4)]
        return (x, dy, grads, scaled_hidden), jnp.stack([mine[0], mine[2]]), jnp.stack([mine[1], mine[3]])

    def over_core(kept, sent):
        got = swap(sent, "tensor", 1)
        return add(kept[0], got[0]), add(kept[1], got[1])

    z2 = swap(own, "expert", 2)
    z1 = swap(own, "expert", 1)
    far0 = swap(own, "tensor", 2)
    near0 = swap(own, "tensor", 1)
    far2 = swap(z2, "tensor", 2)
    z3 = swap(z2, "expert", 1)
    near2 = swap(z2, "tensor", 1)
    far0 = after(far0, z2)
    diagonal0 = swap(far0, "tensor", 1)
    data0, kept0, sent0 = forward(own, near0, far0, diagonal0)
    far2 = after(far2, sent0[0])
    far3 = swap(far2, "expert", 1)
    diagonal2 = swap(far2, "tensor", 1)
    z1 = after(z1, far2)
    far1 = swap(z1, "tensor", 2)
    near1 = swap(z1, "tensor", 1)
    data2, kept2, sent2 = forward(z2, near2, far2, after(diagonal2, z1))
    kept0, sent0 = over_core(kept0, jnp.stack([after(sent0[0], sent2[0]), sent0[1]]))
    kept2, sent2 = over_core(kept2, sent2)
    got2 = swap(sent2, "tensor", 2)
    sent0 = after(sent0, sent2)
    got0 = swap(sent0, "tensor", 2)
    z3 = after(z3, sent2)
    near3 = swap(z3, "tensor", 1)
    far1 = after(far1, sent0)
    diagonal1 = swap(far1, "tensor", 1)
    far3 = after(far3, far1)
    diagonal3 = swap(far3, "tensor", 1)
    data1, kept1, sent1 = forward(z1, near1, far1, after(diagonal1, far3))
    kept1, sent1 = over_core(kept1, sent1)
    got1 = swap(sent1, "tensor", 2)
    data3, kept3, sent3 = forward(z3, near3, after(far3, data1[3]), diagonal3)
    kept3, sent3 = over_core(kept3, sent3)
    got3 = swap(sent3, "tensor", 2)
    sum2 = add(kept2, after(got2, sent3))
    back2 = swap(sum2, "expert", 2)
    sum1 = add(kept1, after(got1, sum2))
    back1 = swap(sum1, "expert", 1)
    sum3 = add(kept3, after(got3, sum1))
    back3 = swap(sum3, "expert", 3)
    got0 = after(got0, sum3)

    parts = lax.optimization_barrier((data0, data1, data2, data3))

    def joined(i):
        return jnp.concatenate([p[i] for p in parts], axis=1)

    x, dy = joined(0), joined(1)
    grads, scaled = after(joined(2), sum2), after(joined(3), sum3)
    ups = after(grads[width:], sum3)
    grad_gate = lax.dot_general(x, grads[:width], lanes, preferred_element_type=F32).astype(BF16)
    grad_up = lax.dot_general(x, ups, lanes, preferred_element_type=F32).astype(BF16)
    grad_down = lax.dot_general(scaled, dy, lanes, preferred_element_type=F32).astype(BF16)
    grad_tokens = add(kept0, got0).astype(F32)
    grad_tokens = (grad_tokens + back1.astype(F32) + back2.astype(F32) + back3.astype(F32)).astype(BF16).T
    return (grad_tokens, grad_gate[None], grad_up[None], grad_down[None])


def solution(mesh):
    placed = (
        P(("groups", "expert"), "tensor"),
        P(("groups", "expert"), "tensor"),
        P(("groups", "expert"), None),
        P(("groups", "expert"), None),
        P("expert", None, "tensor"),
        P("expert", None, "tensor"),
        P("expert", "tensor", None),
    )
    return jax.shard_map(
        per_device,
        mesh=mesh,
        in_specs=placed,
        out_specs=(
            P(("groups", "expert"), "tensor"),
            P(("groups", "expert"), None, "tensor"),
            P(("groups", "expert"), None, "tensor"),
            P(("groups", "expert"), "tensor", None),
        ),
        check_vma=False,
    )
```

```python
import jax
import jax.numpy as jnp
from jax import lax
from jax.sharding import PartitionSpec as P


def per_device_routed(tokens, out_grad, routes, route_probs, w_gate, w_up, w_down):
    expert_count = lax.axis_size("expert")
    token_count, route_count = routes.shape
    route_total = token_count * route_count
    capacity = 2 * route_total
    slot_size = capacity // expert_count
    flat_ids = routes.reshape(-1)
    onehot = (flat_ids[:, None] == jnp.arange(expert_count, dtype=jnp.int32)[None, :]).astype(
        jnp.int32
    )
    before = jnp.cumsum(onehot, axis=0) - onehot
    position = jnp.sum(before * onehot, axis=1)
    slot_of_route = flat_ids * slot_size + position
    route_of_slot = (
        jnp.full((capacity,), route_total, jnp.int32)
        .at[slot_of_route]
        .set(jnp.arange(route_total, dtype=jnp.int32))
    )
    token_of_slot = route_of_slot // route_count
    weights_send = jnp.take(
        jnp.concatenate([route_probs.reshape(-1), jnp.zeros((1,), route_probs.dtype)]),
        route_of_slot,
        axis=0,
    )

    def spread(block_rows):
        padded = jnp.concatenate(
            [block_rows, jnp.zeros((1, block_rows.shape[1]), block_rows.dtype)]
        )
        return jnp.take(padded, token_of_slot, axis=0)

    full_x, full_dy = (
        lax.all_gather(tokens, "tensor", axis=1, tiled=True),
        lax.all_gather(out_grad, "tensor", axis=1, tiled=True),
    )
    rows_x, rows_dy, rows_weight = (
        lax.all_to_all(spread(full_x), "expert", split_axis=0, concat_axis=0, tiled=True),
        lax.all_to_all(spread(full_dy), "expert", split_axis=0, concat_axis=0, tiled=True),
        lax.all_to_all(weights_send, "expert", split_axis=0, concat_axis=0, tiled=True),
    )
    gate_weight = w_gate[0]
    up_weight = w_up[0]
    down_weight = w_down[0]
    contract_last = (((1,), (1,)), ((), ()))
    contract_rows = (((0,), (0,)), ((), ()))
    weight_row = rows_weight.astype(jnp.float32)[:, None]
    pre_gate = jnp.dot(rows_x, gate_weight, preferred_element_type=jnp.float32)
    pre_up = jnp.dot(rows_x, up_weight, preferred_element_type=jnp.float32)
    hidden_grad = (
        lax.dot_general(rows_dy, down_weight, contract_last, preferred_element_type=jnp.float32)
        * weight_row
    )
    sigmoid_gate = jax.nn.sigmoid(pre_gate)
    activated = pre_gate * sigmoid_gate
    hidden = activated * pre_up
    grad_gate_pre = (
        hidden_grad * pre_up * sigmoid_gate * (1.0 + pre_gate * (1.0 - sigmoid_gate))
    ).astype(jnp.bfloat16)
    grad_up_pre = (hidden_grad * activated).astype(jnp.bfloat16)
    scaled_hidden = (hidden * weight_row).astype(jnp.bfloat16)
    partials = lax.dot_general(
        grad_gate_pre, gate_weight, contract_last, preferred_element_type=jnp.float32
    )
    partials = partials + lax.dot_general(
        grad_up_pre, up_weight, contract_last, preferred_element_type=jnp.float32
    )
    partials = partials.astype(jnp.bfloat16)
    summed = (
        lax.psum_scatter(partials, "tensor", scatter_dimension=1, tiled=True)
        .astype(jnp.float32)
        .astype(jnp.bfloat16)
    )
    returned = lax.all_to_all(summed, "expert", split_axis=0, concat_axis=0, tiled=True)
    per_route = (
        jnp.take(returned, slot_of_route, axis=0)
        .astype(jnp.float32)
        .reshape(token_count, route_count, -1)
    )
    grad_tokens = jnp.sum(per_route, axis=1).astype(jnp.bfloat16)
    grad_gate = lax.dot_general(
        rows_x, grad_gate_pre, contract_rows, preferred_element_type=jnp.float32
    ).astype(jnp.bfloat16)
    grad_up = lax.dot_general(
        rows_x, grad_up_pre, contract_rows, preferred_element_type=jnp.float32
    ).astype(jnp.bfloat16)
    grad_down = lax.dot_general(
        scaled_hidden, rows_dy, contract_rows, preferred_element_type=jnp.float32
    ).astype(jnp.bfloat16)
    return (grad_tokens, grad_gate[None], grad_up[None], grad_down[None])


F32 = jnp.float32
BF16 = jnp.bfloat16


def swap(block, axis, bit):
    size = lax.axis_size(axis)
    return lax.ppermute(block, axis, [(i, i ^ bit) for i in range(size)])


def in_order(pieces, me):
    stacked = jnp.stack(pieces)
    return jnp.concatenate(
        [lax.dynamic_index_in_dim(stacked, me ^ t, 0, keepdims=False) for t in range(len(pieces))]
    )


def add(a, b):
    return (a.astype(F32) + b.astype(F32)).astype(BF16)


def after(value, *others):
    head = value[:16].astype(F32)
    for other in others:
        zero = other[:16, :1].astype(F32)
        head = head + jnp.where(zero > 3e38, zero, 0.0)
    return lax.dynamic_update_slice(value, head.astype(value.dtype), (0,) * value.ndim)


def per_device(tokens, out_grad, routes, route_probs, w_gate, w_up, w_down):
    experts, partners = lax.axis_size("expert"), lax.axis_size("tensor")
    token_count, route_count = routes.shape
    if experts != 4 or partners != 4:
        return per_device_routed(tokens, out_grad, routes, route_probs, w_gate, w_up, w_down)
    width = tokens.shape[1]
    me = lax.axis_index("tensor")
    here = lax.axis_index("expert")

    ids, probs = routes.T[:, None, :], route_probs.T[:, None, :]
    expert = lax.broadcasted_iota(jnp.int32, (route_count, 16, token_count), 1)
    weights = jnp.sum(jnp.where(ids == expert, probs, jnp.zeros((), BF16)), axis=0)
    own = jnp.concatenate([tokens.T, out_grad.T, weights])

    gate, up, down = w_gate[0], w_up[0], w_down[0]
    both = jnp.concatenate([gate, up], axis=1)
    first = (((0,), (0,)), ((), ()))
    lanes = (((1,), (1,)), ((), ()))

    def forward(block, near, far, diagonal):
        pieces = (block, near, far, diagonal)
        x = in_order([p[:width] for p in pieces], me)
        dy = in_order([p[width : 2 * width] for p in pieces], me)
        weight = lax.dynamic_slice_in_dim(block, 2 * width + here, 1, 0).astype(F32)
        pre_gate = lax.dot_general(gate, x, first, preferred_element_type=F32)
        pre_up = lax.dot_general(up, x, first, preferred_element_type=F32)
        hidden_grad = jnp.dot(down, dy, preferred_element_type=F32) * weight
        sigmoid_gate = jax.nn.sigmoid(pre_gate)
        activated = pre_gate * sigmoid_gate
        grad_gate_pre = (
            hidden_grad * pre_up * sigmoid_gate * (1.0 + pre_gate * (1.0 - sigmoid_gate))
        ).astype(BF16)
        grad_up_pre = (hidden_grad * activated).astype(BF16)
        scaled_hidden = (activated * pre_up * weight).astype(BF16)
        grads = jnp.concatenate([grad_gate_pre, grad_up_pre])
        partial = jnp.dot(both, grads, preferred_element_type=F32).astype(BF16)
        partial = partial.reshape(partners, width, token_count)
        mine = [lax.dynamic_index_in_dim(partial, me ^ k, 0, keepdims=False) for k in range(4)]
        return (x, dy, grads, scaled_hidden), jnp.stack([mine[0], mine[2]]), jnp.stack([mine[1], mine[3]])

    def over_core(kept, sent):
        got = swap(sent, "tensor", 1)
        return add(kept[0], got[0]), add(kept[1], got[1])

    z2 = swap(own, "expert", 2)
    z1 = swap(own, "expert", 1)
    far0 = swap(own, "tensor", 2)
    near0 = swap(own, "tensor", 1)
    far2 = swap(z2, "tensor", 2)
    z3 = swap(z2, "expert", 1)
    near2 = swap(z2, "tensor", 1)
    far0 = after(far0, z2)
    diagonal0 = swap(far0, "tensor", 1)
    data0, kept0, sent0 = forward(own, near0, far0, diagonal0)
    far2 = after(far2, sent0[0])
    far3 = swap(far2, "expert", 1)
    diagonal2 = swap(far2, "tensor", 1)
    z1 = after(z1, far2)
    far1 = swap(z1, "tensor", 2)
    near1 = swap(z1, "tensor", 1)
    data2, kept2, sent2 = forward(z2, near2, far2, after(diagonal2, z1))
    kept0, sent0 = over_core(kept0, jnp.stack([after(sent0[0], sent2[0]), sent0[1]]))
    kept2, sent2 = over_core(kept2, sent2)
    got2 = swap(sent2, "tensor", 2)
    z3 = after(z3, sent2)
    near3 = swap(z3, "tensor", 1)
    far3 = after(far3, sent2)
    diagonal3 = swap(far3, "tensor", 1)
    far1 = after(far1, far3)
    diagonal1 = swap(far1, "tensor", 1)
    data3, kept3, sent3 = forward(z3, near3, far3, diagonal3)
    data1, kept1, sent1 = forward(z1, near1, far1, after(diagonal1, sent3[0]))
    kept3, sent3 = over_core(kept3, sent3)
    got3 = swap(sent3, "tensor", 2)
    kept1, sent1 = over_core(kept1, sent1)
    sum2 = add(kept2, after(got2, sent3))
    back2 = swap(sum2, "expert", 2)
    got1 = swap(after(sent1, sum2), "tensor", 2)

    parts = lax.optimization_barrier((data0, data1, data2, data3))

    def joined(i):
        return jnp.concatenate([p[i] for p in parts], axis=1)

    def product(a, b):
        return lax.dot_general(a, b, lanes, preferred_element_type=F32).astype(BF16)

    x, dy = joined(0), joined(1)
    grads = joined(2)
    grad_gate = product(x, after(grads[:width], sum2))
    sum3 = add(kept3, after(got3, grad_gate))
    back3 = swap(sum3, "expert", 3)
    sum1 = add(kept1, after(got1, sum3))
    back1 = swap(sum1, "expert", 1)
    got0 = swap(after(sent0, sum3), "tensor", 2)
    grad_up = product(x, after(grads[width:], sum1))
    grad_down = product(after(joined(3), sum1), dy)
    grad_tokens = add(kept0, got0).astype(F32)
    grad_tokens = (grad_tokens + back1.astype(F32) + back2.astype(F32) + back3.astype(F32)).astype(BF16).T
    return (grad_tokens, grad_gate[None], grad_up[None], grad_down[None])


def solution(mesh):
    placed = (
        P(("groups", "expert"), "tensor"),
        P(("groups", "expert"), "tensor"),
        P(("groups", "expert"), None),
        P(("groups", "expert"), None),
        P("expert", None, "tensor"),
        P("expert", None, "tensor"),
        P("expert", "tensor", None),
    )
    return jax.shard_map(
        per_device,
        mesh=mesh,
        in_specs=placed,
        out_specs=(
            P(("groups", "expert"), "tensor"),
            P(("groups", "expert"), None, "tensor"),
            P(("groups", "expert"), None, "tensor"),
            P(("groups", "expert"), "tensor", None),
        ),
        check_vma=False,
    )
```
